1024 devices in a mesh: edp: 16 (over z, core), ep: 64 (over y, x).
Axes of the slice: x: 8, y: 8, z: 8, core: 2. Of those that a mesh axis runs over, the one named last changes fastest.
Arguments:
- tokens: bfloat16 [8192, 4096], P('ep', 'edp'), may hold values from -16 to 16
- router_weight: bfloat16 [4096, 64], P('edp'), may hold values from -0.09375 to 0.09375
- expert_ids: int32 [8192, 8], P('ep'), may hold values from 0 to 63, all different within a row; in each aligned block of 128 rows (0 to 127, 128 to 255, ...) at most 24 rows name the same one
- down_weight: bfloat16 [64, 768, 4096], P('ep', None, 'edp'), may hold values from -0.21875 to 0.21875
- expert_hidden: bfloat16 [64, 1536, 768], P('ep'), may hold values from -6 to 6
- out_grad: bfloat16 [8192, 4096], P('ep', 'edp'), may hold values from -2 to 2
Outputs:
- grad_down: float32 [64, 4096, 768], P('ep', 'edp')
- grad_hidden: bfloat16 [64, 1536, 768], P('ep', 'edp')
- grad_router: float32 [4096, 64], P(('edp', 'ep'))
- grad_tokens: bfloat16 [8192, 4096], P('ep', 'edp')
The draws below stay inside these ranges and needn't reach their ends.
Inputs may be any that keep to these rules, and one draw needn't show every extreme that they name: `expert_ids`: each token names 8 different experts; the 128 tokens of one ep index name any one expert at most 24 times, and in every draw some ep index names some expert exactly 24 times.
All inputs are finite; a program needn't handle non-finite values.
Results may differ from the reference program's by a relative error of at most 0.0049.
Values may be sent and summed in bfloat16 or wider, within the bound.
A program may use at most 32 MiB of HBM per device.

```python
import math
import jax
import jax.numpy as jnp
import numpy as np
from jax import lax

D = 4096
FFW = 768
TOP = 8
TOK_DEV = 128
EXPERTS = 64
CAP = 24
SLOTS = 1536
TOKENS = 8192
N_EP = 64


def with_spikes(array, stream_key, source, target, parts, factor):
    def block_of(dim):
        return (jnp.arange(array.shape[dim]) // (array.shape[dim] // parts)).reshape((-1,) + (1,) * (array.ndim - 1 - dim))

    first = jax.random.permutation(stream_key, parts)[block_of(target)]
    second = (block_of(target) + parts // 2) % parts
    return jnp.where((block_of(source) == first) | (block_of(source) == second), factor * array, array)


def shard_levels(stream_key, shape, pieces, smallest, largest):
    factor_of = 1.0
    for dim, blocks in pieces:
        draws = jax.random.uniform(jax.random.fold_in(jax.random.fold_in(stream_key, 6), dim), (blocks,), jnp.float32, smallest / len(pieces), largest / len(pieces))
        factor_of = factor_of * jnp.repeat(jnp.exp(draws), shape[dim] // blocks).reshape((-1,) + (1,) * (len(shape) - 1 - dim))
    return factor_of


def assign_block(own_key, own, number, rows, count, top, bound, skew):
    order = jax.random.permutation(own_key, count)
    crowded, usual = load_shares(count, rows * top, bound, skew, True), load_shares(count, rows * top, bound, skew, False)
    places = jnp.arange(count)

    def named(tallies, offset_by):
        used = int((tallies > 0).sum())
        fixed = max(1, used // 4)
        moved = fixed + (places - fixed + offset_by * (used - fixed)) % max(1, count - fixed)
        return jnp.zeros((count,), jnp.int32).at[order[jnp.where(places < fixed, places, moved)]].set(jnp.asarray(tallies, jnp.int32))

    tallies = jnp.where(number % 4 == 0, named(crowded, number // 4), named(usual, number - number // 4 - 1))
    mixed = jax.random.permutation(jax.random.fold_in(own, 3), count)
    giver, taker = mixed[0:count // 2 * 2:2], mixed[1:count // 2 * 2:2]
    slack = jnp.minimum(tallies[giver] - 1, bound - tallies[taker]) // 2
    slack = jnp.where((giver == order[0]) | (taker == order[0]) | (tallies[taker] == 0), 0, jnp.maximum(slack, 0))
    moved = jax.random.randint(jax.random.fold_in(own, 4), (count // 2,), 0, 1 << 20) % (slack + 1)
    tallies = tallies.at[giver].add(-moved).at[taker].add(moved)
    labels = jnp.searchsorted(jnp.cumsum(tallies), jnp.arange(rows * top), side="right").astype(jnp.int32)
    table = labels.reshape(top, rows).T
    table = table[jax.random.permutation(jax.random.fold_in(own, 1), rows)]
    offset_by = jax.random.randint(jax.random.fold_in(own, 2), (rows, 1), 0, top)
    return jnp.take_along_axis(table, (jnp.arange(top)[None, :] + offset_by) % top, axis=1)


def load_shares(count, total, most, skew, full):
    loads = [(1 << 20) // math.isqrt(grade ** skew) + 1 for grade in range(1, count + 1)]
    largest = most if full else min(most, max(-(-total // count), total * loads[0] // sum(loads)))
    least = 1 if total - largest >= count - 1 else 0
    given, surplus = [largest] + [least] * (count - 1), total - largest - least * (count - 1)
    while surplus > 0:
        free = [i for i in range(1, count) if given[i] < largest] or [i for i in range(1, count) if given[i] < most]
        mass, left = sum([loads[i] for i in free]), surplus
        for i in free:
            more = min(most - given[i], max(1, left * loads[i] // mass), surplus)
            given[i] = given[i] + more
            surplus = surplus - more
    return np.array(given)


def normal_values(key, dims, spread, limit, shards=(), held_as=jnp.bfloat16):
    entries = jax.random.normal(key, dims, jnp.float32) * spread
    if len(shards) > 0:
        entries = shard_levels(key, dims, shards, -0.22, 0.18) * entries
    return jnp.clip(entries, min=-limit, max=limit).astype(held_as)


def gaussian_with(own_key, shape, width, limit, shards, heavy, held_as=jnp.bfloat16):
    array = width * jax.random.normal(own_key, shape, jnp.float32)
    if shards:
        array = array * shard_levels(own_key, shape, shards, -0.22, 0.18)
    return jnp.clip(with_spikes(array, jax.random.fold_in(own_key, 3), *heavy), -limit, limit).astype(held_as)


def setup_inputs(seed: int = 0) -> dict:
    key_of = jax.random.split(jax.random.key(seed), 7)
    tokens = gaussian_with(key_of[0], (TOKENS, D), 1.0, 16.0, ((0, 64), (1, 16)), (0, 1, 64, 4.0))
    router_weight = normal_values(key_of[1], (D, EXPERTS), D ** -0.5, 0.09375, ((0, 16),))
    expert_ids_keys = jax.random.split(jax.random.fold_in(key_of[2], 1), TOKENS // TOK_DEV)
    expert_ids_turns = jax.random.permutation(jax.random.fold_in(key_of[2], 3), TOKENS // TOK_DEV)
    expert_ids = jax.vmap(lambda own, number: assign_block(jax.random.fold_in(key_of[2], 2), own, number, TOK_DEV, EXPERTS, TOP, CAP, 2))(expert_ids_keys, expert_ids_turns).reshape((TOKENS, TOP))
    down_weight = normal_values(key_of[3], (EXPERTS, FFW, D), FFW ** -0.5, 0.21875, ((0, 64), (2, 16)))
    expert_hidden = normal_values(key_of[4], (EXPERTS, SLOTS, FFW), 1.0, 6.0, ((0, 64),))
    out_grad = normal_values(key_of[5], (TOKENS, D), 0.125, 2.0, ((0, 64), (1, 16)))
    return dict(tokens=tokens, router_weight=router_weight, expert_ids=expert_ids, down_weight=down_weight, expert_hidden=expert_hidden, out_grad=out_grad)


def reference(tokens, router_weight, expert_ids, down_weight, expert_hidden, out_grad):
    logits = jnp.dot(tokens, router_weight, preferred_element_type=jnp.float32)
    expert_range = jnp.arange(EXPERTS, dtype=jnp.int32)
    selector = (expert_ids[:, :, None] == expert_range).astype(jnp.float32)
    picked = jnp.sum(selector * logits[:, None, :], axis=2)
    raised = jnp.exp(picked)
    route_probs = raised / jnp.sum(raised, axis=1, keepdims=True)
    sent_probs = route_probs.astype(jnp.bfloat16)
    pick_count = TOK_DEV * TOP
    group_ids = expert_ids.reshape(N_EP, pick_count)
    counted = (group_ids[:, :, None] == expert_range).astype(jnp.int32)
    slot_rank = jnp.sum((jnp.cumsum(counted, axis=1) - 1) * counted, axis=2).astype(jnp.int32)
    group_index = jnp.broadcast_to(jnp.arange(N_EP, dtype=jnp.int32)[:, None], (N_EP, pick_count))
    token_index = jnp.broadcast_to((jnp.arange(pick_count, dtype=jnp.int32) // TOP)[None, :], (N_EP, pick_count))
    token_table = jnp.full((N_EP, EXPERTS, CAP), -1, jnp.int32).at[group_index, group_ids, slot_rank].set(token_index)
    prob_table = jnp.zeros((N_EP, EXPERTS, CAP), jnp.float32).at[group_index, group_ids, slot_rank].set(
        sent_probs.reshape(N_EP, pick_count).astype(jnp.float32))
    grads_by_group = out_grad.reshape(N_EP, TOK_DEV, D)

    def one_expert(inputs):
        token_rows, prob_rows, weight, hidden_rows = inputs
        filled = token_rows >= 0
        safe_rows = jnp.where(filled, token_rows, 0).astype(jnp.int32)
        gathered = jnp.take_along_axis(grads_by_group, safe_rows[:, :, None], axis=1)
        gathered = jnp.where(filled[:, :, None], gathered, jnp.zeros_like(gathered))
        flat_grad = gathered.reshape(SLOTS, D)
        flat_prob = prob_rows.reshape(SLOTS, 1)
        backward = lax.dot_general(flat_grad, weight, (((1,), (1,)), ((), ())), preferred_element_type=jnp.float32)
        pick_score = jnp.sum(backward * hidden_rows.astype(jnp.float32), axis=1)
        hidden_grad = (flat_prob * backward).astype(jnp.bfloat16)
        scaled = (flat_prob * flat_grad.astype(jnp.float32)).astype(jnp.bfloat16)
        weight_grad = lax.dot_general(scaled, hidden_rows, (((0,), (0,)), ((), ())),
                                      preferred_element_type=jnp.float32)
        return weight_grad, pick_score.reshape(N_EP, CAP), hidden_grad

    grad_down, score_table, grad_hidden = lax.map(
        one_expert, (token_table.transpose(1, 0, 2), prob_table.transpose(1, 0, 2), down_weight, expert_hidden))
    pick_scores = score_table[group_ids, group_index, slot_rank].reshape(TOKENS, TOP)
    centered = route_probs * (pick_scores - jnp.sum(route_probs * pick_scores, axis=1, keepdims=True))
    logit_grad = jnp.sum(selector * centered[:, :, None], axis=1)
    grad_router = lax.dot_general(tokens.astype(jnp.float32), logit_grad, (((0,), (0,)), ((), ())),
                                  precision=lax.Precision.HIGHEST, preferred_element_type=jnp.float32)
    grad_tokens = lax.dot_general(logit_grad, router_weight.astype(jnp.float32), (((1,), (1,)), ((), ())),
                                  precision=lax.Precision.HIGHEST,
                                  preferred_element_type=jnp.float32).astype(jnp.bfloat16)
    return grad_down, grad_hidden, grad_router, grad_tokens
```

```python
import functools
import math

import jax
import jax.numpy as jnp
from jax import lax
from jax.experimental import pallas as pl
from jax.experimental.pallas import tpu as pltpu
from jax.sharding import PartitionSpec as P

F32 = jnp.float32
BF16 = jnp.bfloat16
NN = (((1,), (0,)), ((), ()))
NT = (((1,), (1,)), ((), ()))
TN = (((0,), (0,)), ((), ()))


def matmul(a, b, dims):
    return lax.dot_general(a, b, dims, preferred_element_type=F32)


def split(a):
    high = a.astype(BF16)
    rest = a - high.astype(F32)
    middle = rest.astype(BF16)
    return high, middle, (rest - middle.astype(F32)).astype(BF16)


def push(src, dst, send, recv, device):
    pltpu.make_async_remote_copy(
        src_ref=src,
        dst_ref=dst,
        send_sem=send,
        recv_sem=recv,
        device_id=device,
        device_id_type=pl.DeviceIdType.MESH,
    ).start()


def drain(ref, sem):
    pltpu.make_async_copy(ref, ref, sem).wait()


def kernel(
    side,
    cap,
    tok,
    rwt,
    idt,
    w_any,
    h_any,
    grad,
    down_o,
    hid_o,
    router_o,
    gtok_o,
    w,
    h,
    rank_s,
    gsend,
    grecv,
    psend,
    precv,
    ysend,
    yrecv,
    lsend,
    lrecv,
    fsend,
    frecv,
    back_s,
    own,
    own_total,
    xsend,
    xrecv,
    zsend,
    zrecv,
    pcol_s,
    scaled,
    rsend,
    rrecv,
    load_sem,
    l_sem,
    g_send,
    g_recv,
    p_send,
    p_recv,
    y_sem,
    f_sem,
    x_send,
    x_recv,
    z_sem,
    r_sem,
):
    q, e = lax.axis_index("edp"), lax.axis_index("ep")
    z, c = q // 2, q % 2
    y, x = e // side, e % side
    ep, edp = lax.axis_size("ep"), lax.axis_size("edp")
    rows = ep // side
    top, count = idt.shape
    width = tok.shape[1]
    group = side * cap
    share = group // 2

    load_w = pltpu.make_async_copy(w_any, w, load_sem.at[0])
    load_h = pltpu.make_async_copy(h_any, h, load_sem.at[1])
    load_w.start()
    load_h.start()

    barrier = pltpu.get_barrier_semaphore()

    @pl.loop(1, ep)
    def _(i):
        pl.semaphore_signal(
            barrier, inc=1, device_id=(q, (e + i) % ep), device_id_type=pl.DeviceIdType.MESH
        )

    @pl.loop(1, edp)
    def _(i):
        pl.semaphore_signal(
            barrier, inc=1, device_id=((q + i) % edp, e), device_id_type=pl.DeviceIdType.MESH
        )

    expert = lax.broadcasted_iota(jnp.int32, (ep, count), 0)
    slot = lax.broadcasted_iota(jnp.int32, (side, cap, count), 1).astype(F32)

    def select(k, values):
        return jnp.where(idt[k : k + 1, :] == expert, values, 0.0)

    def to_picks(values):
        return jnp.concatenate(
            [jnp.sum(select(k, values), axis=0, keepdims=True) for k in range(top)], axis=0
        )

    def to_experts(values):
        return sum(select(k, values[k : k + 1, :]) for k in range(top))

    def placement(ranks):
        spread = jnp.broadcast_to(ranks[:, None, :], (side, cap, count))
        return jnp.where(spread == slot, 1.0, 0.0).astype(F32).reshape(group, count)

    lsend[...] = to_picks(matmul(rwt[...], tok[...], NT))
    lrecv[q] = lsend[...]
    named = to_experts(jnp.ones((top, count), F32))
    before = (
        lax.broadcasted_iota(jnp.int32, (count, count), 0)
        < lax.broadcasted_iota(jnp.int32, (count, count), 1)
    ).astype(F32)
    rank = jnp.where(
        named > 0.0, matmul(named.astype(BF16), before.astype(BF16), NN), -1.0
    )
    rank_s[...] = rank

    pl.semaphore_wait(barrier, ep - 1 + edp - 1)

    @pl.loop(1, edp)
    def _(i):
        push(lsend, lrecv.at[q], l_sem.at[0], l_sem.at[1], ((q + i) % edp, e))

    def exchange(row, src, dst, send, recv):
        @pl.loop(0, side)
        def _(dx):
            other = row * side + (x + dx) % side

            @pl.when(other == e)
            def _():
                pltpu.make_async_copy(src.at[other], dst.at[e], recv).start()

            @pl.when(other != e)
            def _():
                push(src.at[other], dst.at[e], send, recv, (q, other))

    def offset(i):
        return (i - z + rows) % rows

    @pl.loop(0, rows)
    def _(i):
        row = (y + offset(i)) % rows
        first = pl.multiple_of(row * side, side)
        place = placement(rank_s[pl.ds(first, side), :]).astype(BF16)
        picked = matmul(place, grad[...], NN)
        gsend[pl.ds(first, side)] = picked.reshape(side, cap, width).astype(BF16)
        exchange(row, gsend, grecv, g_send, g_recv.at[i])

    drain(lrecv.at[pl.ds(0, edp - 1)], l_sem.at[1])
    raised = jnp.exp(sum(lrecv[j] for j in range(edp)))
    probs = raised / jnp.sum(raised, axis=0, keepdims=True)
    sent = to_experts(probs.astype(BF16).astype(F32))
    psend[:, 0, :] = jnp.concatenate([sent, rank], axis=1)

    @pl.loop(0, rows)
    def _(i):
        exchange((y + offset(i)) % rows, psend, precv, p_send, p_recv.at[i])

    load_w.wait()
    load_h.wait()

    def forward(i):
        row = (y - offset(i) + rows) % rows
        drain(xrecv.at[i], x_recv.at[i])
        total = own[i] + xrecv[i].astype(F32)

        @pl.when(row == z)
        def _():
            own_total[...] = total

        @pl.when(row != z)
        def _():
            zsend[i] = total.astype(BF16)
            push(zsend.at[i], zrecv.at[z], z_sem.at[0], z_sem.at[1], (row * 2 + c, e))

    @pl.loop(0, rows)
    def _(i):
        row = (y - offset(i) + rows) % rows
        first = pl.multiple_of(row * side, side)
        start = pl.multiple_of(row * group, group)
        drain(grecv.at[pl.ds(first, side)], g_recv.at[i])
        drain(precv.at[pl.ds(first, side)], p_recv.at[i])
        wide = grecv[pl.ds(first, side)].astype(F32).reshape(group, width)
        back = matmul(wide.astype(BF16), w[...], NT)
        back_s[...] = back
        xsend[i] = back_s[pl.ds(pl.multiple_of((1 - c) * share, share), share), :].astype(BF16)
        push(xsend.at[i], xrecv.at[i], x_send, x_recv.at[i], (z * 2 + 1 - c, e))
        own[i] = back_s[pl.ds(pl.multiple_of(c * share, share), share), :]

        met = precv[pl.ds(first, side), 0, :]
        place = placement(met[:, count:])
        spread = jnp.broadcast_to(met[:, None, :count], (side, cap, count))
        pcol = jnp.sum(place * spread.reshape(group, count), axis=1, keepdims=True)
        score = jnp.sum(back * h[pl.ds(start, group), :].astype(F32), axis=1, keepdims=True)
        ysend[pl.ds(first, side), 0, :] = jnp.sum(
            (place * score).reshape(side, cap, count), axis=1
        )
        exchange(row, ysend, yrecv, y_sem.at[0], y_sem.at[1])
        scaled[pl.ds(start, group), :] = (pcol * wide).astype(BF16)

        @pl.when(row == z)
        def _():
            pcol_s[...] = jnp.broadcast_to(pcol, pcol_s.shape)

        @pl.when(i > 0)
        def _():
            forward(i - 1)

    forward(rows - 1)

    drain(yrecv, y_sem.at[1])
    fsend[...] = to_picks(yrecv[:, 0, :])
    frecv[q] = fsend[...]

    @pl.loop(1, edp)
    def _(i):
        push(fsend, frecv.at[q], f_sem.at[0], f_sem.at[1], ((q + i) % edp, e))

    down_o[...] = matmul(scaled[...], h[...], TN)
    wanted = lax.broadcasted_iota(jnp.int32, (width, width), 0)
    wanted = (wanted % ep) * (width // ep) + wanted // ep
    order = (wanted == lax.broadcasted_iota(jnp.int32, (width, width), 1)).astype(F32)
    turned = matmul(order.astype(BF16), tok[...], NT).astype(BF16)

    drain(frecv.at[pl.ds(0, edp - 1)], f_sem.at[1])
    scores = sum(frecv[j] for j in range(edp))
    centered = probs * (scores - jnp.sum(probs * scores, axis=0, keepdims=True))
    parts = split(to_experts(centered))

    terms = sum(matmul(turned, part, NT) for part in parts)
    rsend[:, 0, :] = jnp.concatenate(
        [terms[j * ep : (j + 1) * ep, :] for j in range(width // ep)], axis=1
    )

    @pl.loop(0, rows)
    def _(i):
        exchange((y + offset(i)) % rows, rsend, rrecv, r_sem.at[0], r_sem.at[1])

    gtok_o[...] = sum(matmul(part, rwt[...], TN) for part in parts).astype(BF16)

    drain(zrecv.at[pl.ds(0, rows - 1)], z_sem.at[1])
    total = own_total[...]
    for j in range(1, rows):
        total = total + zrecv[(z + j) % rows].astype(F32)
    mine = pcol_s[pl.ds(pl.multiple_of(c * share, share), share), :]
    hid_o[...] = (total * mine[:, :1]).astype(BF16)

    drain(rrecv, r_sem.at[1])
    line = jnp.sum(rrecv[...], axis=0)
    for j in range(width // ep):
        router_o[j : j + 1, :] = line[:, j * ep : (j + 1) * ep]

    drain(lrecv.at[pl.ds(0, edp - 1)], l_sem.at[0])
    drain(frecv.at[pl.ds(0, edp - 1)], f_sem.at[0])
    drain(gsend.at[pl.ds(0, ep - 1)], g_send)
    drain(psend.at[pl.ds(0, ep - 1)], p_send)
    drain(ysend.at[pl.ds(0, ep - 1)], y_sem.at[0])
    drain(xsend, x_send)
    drain(zsend.at[pl.ds(0, rows - 1)], z_sem.at[0])
    drain(rsend.at[pl.ds(0, ep - 1)], r_sem.at[0])


def per_device(tokens, router_weight, expert_ids, down_weight, expert_hidden, out_grad):
    count, width = tokens.shape
    top = expert_ids.shape[1]
    ep, edp = lax.axis_size("ep"), lax.axis_size("edp")
    side = math.isqrt(ep)
    rows = ep // side
    slots, ffw = expert_hidden.shape[1:]
    cap = slots // ep
    group = side * cap
    share = slots // edp
    dma = pltpu.SemaphoreType.DMA
    vmem = pl.BlockSpec(memory_space=pltpu.VMEM)
    any_ = pl.BlockSpec(memory_space=pl.ANY)
    down, hidden, router, gtok = pl.pallas_call(
        functools.partial(kernel, side, cap),
        out_shape=(
            jax.ShapeDtypeStruct((width, ffw), F32),
            jax.ShapeDtypeStruct((share, ffw), BF16),
            jax.ShapeDtypeStruct((width // ep, ep), F32),
            jax.ShapeDtypeStruct((count, width), BF16),
        ),
        in_specs=[vmem, vmem, vmem, any_, any_, vmem],
        out_specs=(vmem, vmem, vmem, vmem),
        scratch_shapes=[
            pltpu.VMEM((ffw, width), BF16),
            pltpu.VMEM((slots, ffw), BF16),
            pltpu.VMEM((ep, count), F32),
            pltpu.VMEM((ep, cap, width), BF16),
            pltpu.VMEM((ep, cap, width), BF16),
            pltpu.VMEM((ep, 1, 2 * count), F32),
            pltpu.VMEM((ep, 1, 2 * count), F32),
            pltpu.VMEM((ep, 1, count), F32),
            pltpu.VMEM((ep, 1, count), F32),
            pltpu.VMEM((top, count), F32),
            pltpu.VMEM((edp, top, count), F32),
            pltpu.VMEM((top, count), F32),
            pltpu.VMEM((edp, top, count), F32),
            pltpu.VMEM((group, ffw), F32),
            pltpu.VMEM((rows, share, ffw), F32),
            pltpu.VMEM((share, ffw), F32),
            pltpu.VMEM((rows, share, ffw), BF16),
            pltpu.VMEM((rows, share, ffw), BF16),
            pltpu.VMEM((rows, share, ffw), BF16),
            pltpu.VMEM((rows, share, ffw), BF16),
            pltpu.VMEM((group, 128), F32),
            pltpu.VMEM((slots, width), BF16),
            pltpu.VMEM((ep, 1, width), F32),
            pltpu.VMEM((ep, 1, width), F32),
            dma((2,)),
            dma((2,)),
            dma,
            dma((rows,)),
            dma,
            dma((rows,)),
            dma((2,)),
            dma((2,)),
            dma,
            dma((rows,)),
            dma((2,)),
            dma((2,)),
        ],
        compiler_params=pltpu.CompilerParams(
            collective_id=0, has_side_effects=True, vmem_limit_bytes=48 * 1024 * 1024
        ),
    )(tokens, router_weight.T, expert_ids.T, down_weight[0], expert_hidden[0], out_grad)
    return down[None], hidden[None], router, gtok


def solution(mesh):
    in_specs = (
        P("ep", "edp"),
        P("edp", None),
        P("ep", None),
        P("ep", None, "edp"),
        P("ep", None, None),
        P("ep", "edp"),
    )
    out_specs = (P("ep", "edp", None), P("ep", "edp", None), P(("edp", "ep"), None), P("ep", "edp"))
    return jax.shard_map(
        per_device, mesh=mesh, in_specs=in_specs, out_specs=out_specs, check_vma=False
    )
```

```python
import functools
import math

import jax
import jax.numpy as jnp
from jax import lax
from jax.experimental import pallas as pl
from jax.experimental.pallas import tpu as pltpu
from jax.sharding import PartitionSpec as P

F32 = jnp.float32
BF16 = jnp.bfloat16
NN = (((1,), (0,)), ((), ()))
NT = (((1,), (1,)), ((), ()))
TN = (((0,), (0,)), ((), ()))
EARLY = 4
HELD = 7


def matmul(a, b, dims):
    return lax.dot_general(a, b, dims, preferred_element_type=F32)


def split(a):
    high = a.astype(BF16)
    rest = a - high.astype(F32)
    middle = rest.astype(BF16)
    return high, middle, (rest - middle.astype(F32)).astype(BF16)


def push(src, dst, send, recv, device):
    pltpu.make_async_remote_copy(
        src_ref=src,
        dst_ref=dst,
        send_sem=send,
        recv_sem=recv,
        device_id=device,
        device_id_type=pl.DeviceIdType.MESH,
    ).start()


def drain(ref, sem):
    pltpu.make_async_copy(ref, ref, sem).wait()


def kernel(
    side,
    cap,
    tok_any,
    rwt_any,
    idt_any,
    w_any,
    h_any,
    grad_any,
    down_o,
    hid_o,
    router_o,
    gtok_o,
    tok,
    rwt,
    idt,
    grad,
    w,
    h,
    rank_s,
    probs_s,
    gsend,
    grecv,
    psend,
    pmid,
    precv,
    ysend,
    yrecv,
    lsend,
    lrecv,
    fsend,
    frecv,
    back_s,
    own,
    own_total,
    xsend,
    xrecv,
    zsend,
    zrecv,
    pcol_s,
    scaled,
    rsend,
    rmid,
    rsum,
    rrecv,
    load_sem,
    l_sem,
    g_send,
    g_recv,
    p_sem,
    y_sem,
    f_sem,
    x_send,
    x_recv,
    z_sem,
    r_sem,
):
    q, e = lax.axis_index("edp"), lax.axis_index("ep")
    z, c = q // 2, q % 2
    y, x = e // side, e % side
    ep, edp = lax.axis_size("ep"), lax.axis_size("edp")
    rows = ep // side
    top, count = idt.shape
    width = tok.shape[1]
    group = side * cap
    share = group // 2

    loads = [
        pltpu.make_async_copy(src, dst, load_sem.at[j])
        for j, (src, dst) in enumerate(
            [(idt_any, idt), (tok_any, tok), (rwt_any, rwt), (grad_any, grad), (w_any, w), (h_any, h)]
        )
    ]
    for load in loads:
        load.start()

    barrier = pltpu.get_barrier_semaphore()

    @pl.loop(1, ep)
    def _(i):
        pl.semaphore_signal(
            barrier, inc=1, device_id=(q, (e + i) % ep), device_id_type=pl.DeviceIdType.MESH
        )

    @pl.loop(1, edp)
    def _(i):
        pl.semaphore_signal(
            barrier, inc=1, device_id=((q + i) % edp, e), device_id_type=pl.DeviceIdType.MESH
        )

    for load in loads[:3]:
        load.wait()
    expert = lax.broadcasted_iota(jnp.int32, (ep, count), 0)
    slot = lax.broadcasted_iota(jnp.int32, (side, cap, count), 1).astype(F32)
    lane = lax.broadcasted_iota(jnp.int32, (side, cap, count), 2).astype(F32)
    own_slot = jnp.where(slot == lane, 1.0, 0.0).astype(F32).reshape(group, count)

    def select(k, values):
        return jnp.where(idt[k : k + 1, :] == expert, values, 0.0)

    def to_picks(values):
        return jnp.concatenate(
            [jnp.sum(select(k, values), axis=0, keepdims=True) for k in range(top)], axis=0
        )

    def to_experts(values):
        return sum(select(k, values[k : k + 1, :]) for k in range(top))

    def placement(ranks):
        spread = jnp.broadcast_to(ranks[:, None, :], (side, cap, count))
        return jnp.where(spread == slot, 1.0, 0.0).astype(F32).reshape(group, count)

    lsend[...] = to_picks(matmul(rwt[...], tok[...], NT))
    lrecv[q] = lsend[...]
    named = to_experts(jnp.ones((top, count), F32))
    before = (
        lax.broadcasted_iota(jnp.int32, (count, count), 0)
        < lax.broadcasted_iota(jnp.int32, (count, count), 1)
    ).astype(F32)
    rank = jnp.where(
        named > 0.0, matmul(named.astype(BF16), before.astype(BF16), NN), -1.0
    )
    rank_s[...] = rank

    loads[3].wait()
    pl.semaphore_wait(barrier, ep - 1 + edp - 1)

    @pl.loop(1, edp)
    def _(i):
        push(lsend, lrecv.at[q], l_sem.at[0], l_sem.at[1], ((q + i) % edp, e))

    def exchange(row, src, dst, send, recv):
        @pl.loop(0, side)
        def _(dx):
            other = row * side + (x + 3 * dx) % side

            @pl.when(other == e)
            def _():
                pltpu.make_async_copy(src.at[other], dst.at[e], recv).start()

            @pl.when(other != e)
            def _():
                push(src.at[other], dst.at[e], send, recv, (q, other))

    def offset(i):
        return (3 * i - z + rows) % rows

    def dispatch(i):
        row = (y + offset(i)) % rows
        first = pl.multiple_of(row * side, side)
        place = placement(rank_s[pl.ds(first, side), :]).astype(BF16)
        picked = matmul(place, grad[...], NN)
        gsend[pl.ds(first, side)] = picked.reshape(side, cap, width).astype(BF16)
        exchange(row, gsend, grecv, g_send, g_recv.at[i])

    ahead = min(EARLY, rows)
    pl.loop(0, ahead)(dispatch)

    def weigh():
        drain(lrecv.at[pl.ds(0, edp - 1)], l_sem.at[1])
        raised = jnp.exp(sum(lrecv[j] for j in range(edp)))
        probs = raised / jnp.sum(raised, axis=0, keepdims=True)
        probs_s[...] = probs
        sent = to_experts(probs.astype(BF16).astype(F32))
        psend[...] = jnp.concatenate([sent, rank_s[...]], axis=1).reshape(psend.shape)
        pltpu.make_async_copy(psend.at[y], pmid.at[y], p_sem.at[1]).start()

        @pl.loop(1, rows)
        def _(j):
            other = (y + j) % rows
            push(psend.at[other], pmid.at[y], p_sem.at[0], p_sem.at[1], (q, other * side + x))

    loads[4].wait()
    loads[5].wait()

    def forward(i):
        row = (y - offset(i) + rows) % rows
        drain(xrecv.at[i], x_recv.at[i])
        total = own[i] + xrecv[i].astype(F32)

        @pl.when(row == z)
        def _():
            own_total[...] = total

        @pl.when(row != z)
        def _():
            zsend[i] = total.astype(BF16)
            push(zsend.at[i], zrecv.at[z], z_sem.at[0], z_sem.at[1], (row * 2 + c, e))

    @pl.loop(0, rows)
    def _(i):
        row = (y - offset(i) + rows) % rows
        first = pl.multiple_of(row * side, side)
        start = pl.multiple_of(row * group, group)
        drain(grecv.at[pl.ds(first, side)], g_recv.at[i])
        wide = grecv[pl.ds(first, side)].astype(F32).reshape(group, width)
        back = matmul(wide.astype(BF16), w[...], NT)
        back_s[...] = back
        xsend[i] = back_s[pl.ds(pl.multiple_of((1 - c) * share, share), share), :].astype(BF16)
        push(xsend.at[i], xrecv.at[i], x_send, x_recv.at[i], (z * 2 + 1 - c, e))
        own[i] = back_s[pl.ds(pl.multiple_of(c * share, share), share), :]

        score = jnp.sum(back * h[pl.ds(start, group), :].astype(F32), axis=1, keepdims=True)
        ysend[pl.ds(first, side), 0, :] = jnp.sum(
            (own_slot * score).reshape(side, cap, count), axis=1
        )
        exchange(row, ysend, yrecv, y_sem.at[0], y_sem.at[1])

        @pl.when((i > 0) & (i <= HELD))
        def _():
            forward(i - 1)

        @pl.when(i + ahead < rows)
        def _():
            dispatch(i + ahead)

        @pl.when(i == rows // 2)
        def _():
            weigh()

    drain(yrecv, y_sem.at[1])
    found = yrecv[:, 0, :]
    ranks = rank_s[...]
    spread = sum(jnp.where(ranks == float(j), found[:, j : j + 1], 0.0) for j in range(cap))
    fsend[...] = to_picks(spread)
    frecv[q] = fsend[...]

    @pl.loop(1, edp)
    def _(i):
        push(fsend, frecv.at[q], f_sem.at[0], f_sem.at[1], ((q + i) % edp, e))

    drain(pmid, p_sem.at[1])
    pltpu.make_async_copy(pmid.at[:, x], precv.at[:, x], p_sem.at[3]).start()

    @pl.loop(1, side)
    def _(j):
        other = (x + j) % side
        push(
            pmid.at[:, other], precv.at[:, x], p_sem.at[2], p_sem.at[3], (q, y * side + other)
        )

    pl.loop(min(HELD, rows - 1), rows)(forward)

    wanted = lax.broadcasted_iota(jnp.int32, (width, width), 0)
    wanted = (wanted % ep) * (width // ep) + wanted // ep
    order = (wanted == lax.broadcasted_iota(jnp.int32, (width, width), 1)).astype(F32)
    turned = matmul(order.astype(BF16), tok[...], NT).astype(BF16)

    drain(frecv.at[pl.ds(0, edp - 1)], f_sem.at[1])
    scores = sum(frecv[j] for j in range(edp))
    probs = probs_s[...]
    centered = probs * (scores - jnp.sum(probs * scores, axis=0, keepdims=True))
    parts = split(to_experts(centered))

    terms = sum(matmul(turned, part, NT) for part in parts)
    lines = jnp.concatenate(
        [terms[j * ep : (j + 1) * ep, :] for j in range(width // ep)], axis=1
    )
    rsend[...] = lines.reshape(rsend.shape)

    @pl.loop(1, side)
    def _(j):
        other = (x + j) % side
        push(rsend.at[:, other], rmid.at[x], r_sem.at[0], r_sem.at[1], (q, y * side + other))

    gtok_o[...] = sum(matmul(part, rwt[...], TN) for part in parts).astype(BF16)

    drain(precv, p_sem.at[3])

    @pl.loop(0, rows)
    def _(row):
        first = pl.multiple_of(row * side, side)
        start = pl.multiple_of(row * group, group)
        met = precv[row].reshape(side, 2 * count)
        place = placement(met[:, count:])
        weights = jnp.broadcast_to(met[:, None, :count], (side, cap, count))
        pcol = jnp.sum(place * weights.reshape(group, count), axis=1, keepdims=True)
        wide = grecv[pl.ds(first, side)].astype(F32).reshape(group, width)
        scaled[pl.ds(start, group), :] = (pcol * wide).astype(BF16)

        @pl.when(row == z)
        def _():
            pcol_s[...] = jnp.broadcast_to(pcol, pcol_s.shape)

    drain(rmid.at[pl.ds(0, side - 1)], r_sem.at[1])
    line = rsend[:, x]
    for j in range(1, side):
        line = line + rmid[(x + j) % side]
    rsum[...] = line

    @pl.loop(1, rows)
    def _(j):
        other = (y + j) % rows
        push(rsum.at[other], rrecv.at[y], r_sem.at[2], r_sem.at[3], (q, other * side + x))

    down_o[...] = matmul(scaled[...], h[...], TN)
    drain(zrecv.at[pl.ds(0, rows - 1)], z_sem.at[1])
    total = own_total[...]
    for j in range(1, rows):
        total = total + zrecv[(z + j) % rows].astype(F32)
    mine = pcol_s[pl.ds(pl.multiple_of(c * share, share), share), :]
    hid_o[...] = (total * mine[:, :1]).astype(BF16)

    drain(rrecv.at[pl.ds(0, rows - 1)], r_sem.at[3])
    line = rsum[y]
    for j in range(1, rows):
        line = line + rrecv[(y + j) % rows]
    for j in range(width // ep):
        router_o[j : j + 1, :] = line[:, j * ep : (j + 1) * ep]

    drain(lrecv.at[pl.ds(0, edp - 1)], l_sem.at[0])
    drain(frecv.at[pl.ds(0, edp - 1)], f_sem.at[0])
    drain(gsend.at[pl.ds(0, ep - 1)], g_send)
    drain(psend.at[pl.ds(0, rows - 1)], p_sem.at[0])
    drain(pmid.at[pl.ds(0, side - 1)], p_sem.at[2])
    drain(ysend.at[pl.ds(0, ep - 1)], y_sem.at[0])
    drain(xsend, x_send)
    drain(zsend.at[pl.ds(0, rows - 1)], z_sem.at[0])
    drain(rmid.at[pl.ds(0, side - 1)], r_sem.at[0])
    drain(rrecv.at[pl.ds(0, rows - 1)], r_sem.at[2])


def per_device(tokens, router_weight, expert_ids, down_weight, expert_hidden, out_grad):
    count, width = tokens.shape
    top = expert_ids.shape[1]
    ep, edp = lax.axis_size("ep"), lax.axis_size("edp")
    side = math.isqrt(ep)
    rows = ep // side
    slots, ffw = expert_hidden.shape[1:]
    cap = slots // ep
    group = side * cap
    share = slots // edp
    dma = pltpu.SemaphoreType.DMA
    vmem = pl.BlockSpec(memory_space=pltpu.VMEM)
    any_ = pl.BlockSpec(memory_space=pl.ANY)
    shapes = (
        jax.ShapeDtypeStruct((width, ffw), F32),
        jax.ShapeDtypeStruct((share, ffw), BF16),
        jax.ShapeDtypeStruct((width // ep, ep), F32),
        jax.ShapeDtypeStruct((count, width), BF16),
    )
    down, hidden, router, gtok = pl.pallas_call(
        functools.partial(kernel, side, cap),
        out_shape=shapes,
        in_specs=[any_] * 6,
        out_specs=(vmem, vmem, vmem, vmem),
        scratch_shapes=[
            pltpu.VMEM((count, width), BF16),
            pltpu.VMEM((ep, width), BF16),
            pltpu.VMEM((top, count), jnp.int32),
            pltpu.VMEM((count, width), BF16),
            pltpu.VMEM((ffw, width), BF16),
            pltpu.VMEM((slots, ffw), BF16),
            pltpu.VMEM((ep, count), F32),
            pltpu.VMEM((top, count), F32),
            pltpu.VMEM((ep, cap, width), BF16),
            pltpu.VMEM((ep, cap, width), BF16),
            pltpu.VMEM((rows, side, 1, 2 * count), F32),
            pltpu.VMEM((rows, side, 1, 2 * count), F32),
            pltpu.VMEM((rows, side, 1, 2 * count), F32),
            pltpu.VMEM((ep, 1, count), F32),
            pltpu.VMEM((ep, 1, count), F32),
            pltpu.VMEM((top, count), F32),
            pltpu.VMEM((edp, top, count), F32),
            pltpu.VMEM((top, count), F32),
            pltpu.VMEM((edp, top, count), F32),
            pltpu.VMEM((group, ffw), F32),
            pltpu.VMEM((rows, share, ffw), F32),
            pltpu.VMEM((share, ffw), F32),
            pltpu.VMEM((rows, share, ffw), BF16),
            pltpu.VMEM((rows, share, ffw), BF16),
            pltpu.VMEM((rows, share, ffw), BF16),
            pltpu.VMEM((rows, share, ffw), BF16),
            pltpu.VMEM((group, 128), F32),
            pltpu.VMEM((slots, width), BF16),
            pltpu.VMEM((rows, side, 1, width), F32),
            pltpu.VMEM((side, rows, 1, width), F32),
            pltpu.VMEM((rows, 1, width), F32),
            pltpu.VMEM((rows, 1, width), F32),
            dma((6,)),
            dma((2,)),
            dma,
            dma((rows,)),
            dma((4,)),
            dma((2,)),
            dma((2,)),
            dma,
            dma((rows,)),
            dma((2,)),
            dma((4,)),
        ],
        compiler_params=pltpu.CompilerParams(
            collective_id=0, has_side_effects=True, vmem_limit_bytes=60 * 1024 * 1024
        ),
    )(tokens, router_weight.T, expert_ids.T, down_weight[0], expert_hidden[0], out_grad)
    return down[None], hidden[None], router, gtok


def solution(mesh):
    in_specs = (
        P("ep", "edp"),
        P("edp", None),
        P("ep", None),
        P("ep", None, "edp"),
        P("ep", None, None),
        P("ep", "edp"),
    )
    out_specs = (P("ep", "edp", None), P("ep", "edp", None), P(("edp", "ep"), None), P("ep", "edp"))
    return jax.shard_map(
        per_device, mesh=mesh, in_specs=in_specs, out_specs=out_specs, check_vma=False
    )
```

```python
import functools
import math

import jax
import jax.numpy as jnp
from jax import lax
from jax.experimental import pallas as pl
from jax.experimental.pallas import tpu as pltpu
from jax.sharding import PartitionSpec as P

F32 = jnp.float32
BF16 = jnp.bfloat16
NN = (((1,), (0,)), ((), ()))
NT = (((1,), (1,)), ((), ()))
TN = (((0,), (0,)), ((), ()))
EARLY = 4
HELD = 7


def matmul(a, b, dims):
    return lax.dot_general(a, b, dims, preferred_element_type=F32)


def split(a):
    high = a.astype(BF16)
    rest = a - high.astype(F32)
    middle = rest.astype(BF16)
    return high, middle, (rest - middle.astype(F32)).astype(BF16)


def push(src, dst, send, recv, device):
    pltpu.make_async_remote_copy(
        src_ref=src,
        dst_ref=dst,
        send_sem=send,
        recv_sem=recv,
        device_id=device,
        device_id_type=pl.DeviceIdType.MESH,
    ).start()


def drain(ref, sem):
    pltpu.make_async_copy(ref, ref, sem).wait()


def kernel(
    side,
    cap,
    tok_any,
    rwt_any,
    idt_any,
    w_any,
    h_any,
    grad_any,
    down_o,
    hid_o,
    router_o,
    gtok_o,
    tok,
    rwt,
    idt,
    grad,
    w,
    h,
    rank_s,
    probs_s,
    gsend,
    grecv,
    psend,
    pmid,
    precv,
    ysend,
    yrecv,
    lsend,
    lrecv,
    fsend,
    frecv,
    back_s,
    own,
    own_total,
    xsend,
    xrecv,
    zsend,
    zrecv,
    pcol_s,
    scaled,
    rsend,
    rmid,
    rsum,
    rrecv,
    load_sem,
    l_sem,
    g_send,
    g_recv,
    p_sem,
    y_sem,
    f_sem,
    x_send,
    x_recv,
    z_sem,
    r_sem,
):
    q, e = lax.axis_index("edp"), lax.axis_index("ep")
    z, c = q // 2, q % 2
    y, x = e // side, e % side
    ep, edp = lax.axis_size("ep"), lax.axis_size("edp")
    rows = ep // side
    top, count = idt.shape
    width = tok.shape[1]
    group = side * cap
    share = group // 2

    loads = [
        pltpu.make_async_copy(src, dst, load_sem.at[j])
        for j, (src, dst) in enumerate(
            [(idt_any, idt), (grad_any, grad), (tok_any, tok), (rwt_any, rwt), (w_any, w), (h_any, h)]
        )
    ]
    for load in loads:
        load.start()

    barrier = pltpu.get_barrier_semaphore()

    @pl.loop(1, ep)
    def _(i):
        pl.semaphore_signal(
            barrier, inc=1, device_id=(q, (e + i) % ep), device_id_type=pl.DeviceIdType.MESH
        )

    @pl.loop(1, edp)
    def _(i):
        pl.semaphore_signal(
            barrier, inc=1, device_id=((q + i) % edp, e), device_id_type=pl.DeviceIdType.MESH
        )

    loads[0].wait()
    expert = lax.broadcasted_iota(jnp.int32, (ep, count), 0)
    slot = lax.broadcasted_iota(jnp.int32, (side, cap, count), 1).astype(F32)
    lane = lax.broadcasted_iota(jnp.int32, (side, cap, count), 2).astype(F32)
    own_slot = jnp.where(slot == lane, 1.0, 0.0).astype(F32).reshape(group, count)

    def select(k, values):
        return jnp.where(idt[k : k + 1, :] == expert, values, 0.0)

    def to_picks(values):
        return jnp.concatenate(
            [jnp.sum(select(k, values), axis=0, keepdims=True) for k in range(top)], axis=0
        )

    def to_experts(values):
        return sum(select(k, values[k : k + 1, :]) for k in range(top))

    def placement(ranks):
        spread = jnp.broadcast_to(ranks[:, None, :], (side, cap, count))
        return jnp.where(spread == slot, 1.0, 0.0).astype(F32).reshape(group, count)

    named = to_experts(jnp.ones((top, count), F32))
    before = (
        lax.broadcasted_iota(jnp.int32, (count, count), 0)
        < lax.broadcasted_iota(jnp.int32, (count, count), 1)
    ).astype(F32)
    rank = jnp.where(
        named > 0.0, matmul(named.astype(BF16), before.astype(BF16), NN), -1.0
    )
    rank_s[...] = rank

    loads[1].wait()
    pl.semaphore_wait(barrier, ep - 1 + edp - 1)

    def exchange(row, src, dst, send, recv):
        @pl.loop(0, side)
        def _(dx):
            other = row * side + (x + 3 * dx) % side

            @pl.when(other == e)
            def _():
                pltpu.make_async_copy(src.at[other], dst.at[e], recv).start()

            @pl.when(other != e)
            def _():
                push(src.at[other], dst.at[e], send, recv, (q, other))

    def offset(i):
        return (3 * i - z + rows) % rows

    def dispatch(i):
        row = (y + offset(i)) % rows
        first = pl.multiple_of(row * side, side)
        place = placement(rank_s[pl.ds(first, side), :]).astype(BF16)
        picked = matmul(place, grad[...], NN)
        gsend[pl.ds(first, side)] = picked.reshape(side, cap, width).astype(BF16)
        exchange(row, gsend, grecv, g_send, g_recv.at[i])

    ahead = min(EARLY, rows)
    pl.loop(0, ahead)(dispatch)

    for load in loads[2:4]:
        load.wait()
    lsend[...] = to_picks(matmul(rwt[...], tok[...], NT))
    lrecv[q] = lsend[...]

    @pl.loop(1, edp)
    def _(i):
        push(lsend, lrecv.at[q], l_sem.at[0], l_sem.at[1], ((q + i) % edp, e))

    def weigh():
        drain(lrecv.at[pl.ds(0, edp - 1)], l_sem.at[1])
        raised = jnp.exp(sum(lrecv[j] for j in range(edp)))
        probs = raised / jnp.sum(raised, axis=0, keepdims=True)
        probs_s[...] = probs
        sent = to_experts(probs.astype(BF16).astype(F32))
        psend[...] = jnp.concatenate([sent, rank_s[...]], axis=1).reshape(psend.shape)
        pltpu.make_async_copy(psend.at[y], pmid.at[y], p_sem.at[1]).start()

        @pl.loop(1, rows)
        def _(j):
            other = (y + j) % rows
            push(psend.at[other], pmid.at[y], p_sem.at[0], p_sem.at[1], (q, other * side + x))

    loads[4].wait()
    loads[5].wait()

    def forward(i):
        row = (y - offset(i) + rows) % rows
        drain(xrecv.at[i], x_recv.at[i])
        total = own[i] + xrecv[i].astype(F32)

        @pl.when(row == z)
        def _():
            own_total[...] = total

        @pl.when(row != z)
        def _():
            zsend[i] = total.astype(BF16)
            push(zsend.at[i], zrecv.at[z], z_sem.at[0], z_sem.at[1], (row * 2 + c, e))

    @pl.loop(0, rows)
    def _(i):
        row = (y - offset(i) + rows) % rows
        first = pl.multiple_of(row * side, side)
        start = pl.multiple_of(row * group, group)
        drain(grecv.at[pl.ds(first, side)], g_recv.at[i])
        wide = grecv[pl.ds(first, side)].astype(F32).reshape(group, width)
        back = matmul(wide.astype(BF16), w[...], NT)
        back_s[...] = back
        xsend[i] = back_s[pl.ds(pl.multiple_of((1 - c) * share, share), share), :].astype(BF16)
        push(xsend.at[i], xrecv.at[i], x_send, x_recv.at[i], (z * 2 + 1 - c, e))
        own[i] = back_s[pl.ds(pl.multiple_of(c * share, share), share), :]

        score = jnp.sum(back * h[pl.ds(start, group), :].astype(F32), axis=1, keepdims=True)
        ysend[pl.ds(first, side), 0, :] = jnp.sum(
            (own_slot * score).reshape(side, cap, count), axis=1
        )
        exchange(row, ysend, yrecv, y_sem.at[0], y_sem.at[1])

        @pl.when((i > 0) & (i <= HELD))
        def _():
            forward(i - 1)

        @pl.when(i + ahead < rows)
        def _():
            dispatch(i + ahead)

        @pl.when(i == rows // 2)
        def _():
            weigh()

    drain(yrecv, y_sem.at[1])
    found = yrecv[:, 0, :]
    ranks = rank_s[...]
    spread = sum(jnp.where(ranks == float(j), found[:, j : j + 1], 0.0) for j in range(cap))
    fsend[...] = to_picks(spread)
    frecv[q] = fsend[...]

    @pl.loop(1, edp)
    def _(i):
        push(fsend, frecv.at[q], f_sem.at[0], f_sem.at[1], ((q + i) % edp, e))

    drain(pmid, p_sem.at[1])
    pltpu.make_async_copy(pmid.at[:, x], precv.at[:, x], p_sem.at[3]).start()

    @pl.loop(1, side)
    def _(j):
        other = (x + j) % side
        push(
            pmid.at[:, other], precv.at[:, x], p_sem.at[2], p_sem.at[3], (q, y * side + other)
        )

    pl.loop(min(HELD, rows - 1), rows)(forward)

    wanted = lax.broadcasted_iota(jnp.int32, (width, width), 0)
    wanted = (wanted % ep) * (width // ep) + wanted // ep
    order = (wanted == lax.broadcasted_iota(jnp.int32, (width, width), 1)).astype(F32)
    turned = matmul(order.astype(BF16), tok[...], NT).astype(BF16)

    drain(frecv.at[pl.ds(0, edp - 1)], f_sem.at[1])
    scores = sum(frecv[j] for j in range(edp))
    probs = probs_s[...]
    centered = probs * (scores - jnp.sum(probs * scores, axis=0, keepdims=True))
    parts = split(to_experts(centered))

    terms = sum(matmul(turned, part, NT) for part in parts)
    lines = jnp.concatenate(
        [terms[j * ep : (j + 1) * ep, :] for j in range(width // ep)], axis=1
    )
    rsend[...] = lines.reshape(rsend.shape)

    @pl.loop(1, side)
    def _(j):
        other = (x + j) % side
        push(rsend.at[:, other], rmid.at[x], r_sem.at[0], r_sem.at[1], (q, y * side + other))

    gtok_o[...] = sum(matmul(part, rwt[...], TN) for part in parts).astype(BF16)

    drain(precv, p_sem.at[3])

    @pl.loop(0, rows)
    def _(row):
        first = pl.multiple_of(row * side, side)
        start = pl.multiple_of(row * group, group)
        met = precv[row].reshape(side, 2 * count)
        place = placement(met[:, count:])
        weights = jnp.broadcast_to(met[:, None, :count], (side, cap, count))
        pcol = jnp.sum(place * weights.reshape(group, count), axis=1, keepdims=True)
        wide = grecv[pl.ds(first, side)].astype(F32).reshape(group, width)
        scaled[pl.ds(start, group), :] = (pcol * wide).astype(BF16)

        @pl.when(row == z)
        def _():
            pcol_s[...] = jnp.broadcast_to(pcol, pcol_s.shape)

    drain(rmid.at[pl.ds(0, side - 1)], r_sem.at[1])
    line = rsend[:, x]
    for j in range(1, side):
        line = line + rmid[(x + j) % side]
    rsum[...] = line

    @pl.loop(1, rows)
    def _(j):
        other = (y + j) % rows
        push(rsum.at[other], rrecv.at[y], r_sem.at[2], r_sem.at[3], (q, other * side + x))

    down_o[...] = matmul(scaled[...], h[...], TN)
    drain(zrecv.at[pl.ds(0, rows - 1)], z_sem.at[1])
    total = own_total[...]
    for j in range(1, rows):
        total = total + zrecv[(z + j) % rows].astype(F32)
    mine = pcol_s[pl.ds(pl.multiple_of(c * share, share), share), :]
    hid_o[...] = (total * mine[:, :1]).astype(BF16)

    drain(rrecv.at[pl.ds(0, rows - 1)], r_sem.at[3])
    line = rsum[y]
    for j in range(1, rows):
        line = line + rrecv[(y + j) % rows]
    for j in range(width // ep):
        router_o[j : j + 1, :] = line[:, j * ep : (j + 1) * ep]

    drain(lrecv.at[pl.ds(0, edp - 1)], l_sem.at[0])
    drain(frecv.at[pl.ds(0, edp - 1)], f_sem.at[0])
    drain(gsend.at[pl.ds(0, ep - 1)], g_send)
    drain(psend.at[pl.ds(0, rows - 1)], p_sem.at[0])
    drain(pmid.at[pl.ds(0, side - 1)], p_sem.at[2])
    drain(ysend.at[pl.ds(0, ep - 1)], y_sem.at[0])
    drain(xsend, x_send)
    drain(zsend.at[pl.ds(0, rows - 1)], z_sem.at[0])
    drain(rmid.at[pl.ds(0, side - 1)], r_sem.at[0])
    drain(rrecv.at[pl.ds(0, rows - 1)], r_sem.at[2])


def per_device(tokens, router_weight, expert_ids, down_weight, expert_hidden, out_grad):
    count, width = tokens.shape
    top = expert_ids.shape[1]
    ep, edp = lax.axis_size("ep"), lax.axis_size("edp")
    side = math.isqrt(ep)
    rows = ep // side
    slots, ffw = expert_hidden.shape[1:]
    cap = slots // ep
    group = side * cap
    share = slots // edp
    dma = pltpu.SemaphoreType.DMA
    vmem = pl.BlockSpec(memory_space=pltpu.VMEM)
    any_ = pl.BlockSpec(memory_space=pl.ANY)
    shapes = (
        jax.ShapeDtypeStruct((width, ffw), F32),
        jax.ShapeDtypeStruct((share, ffw), BF16),
        jax.ShapeDtypeStruct((width // ep, ep), F32),
        jax.ShapeDtypeStruct((count, width), BF16),
    )
    down, hidden, router, gtok = pl.pallas_call(
        functools.partial(kernel, side, cap),
        out_shape=shapes,
        in_specs=[any_] * 6,
        out_specs=(vmem, vmem, vmem, vmem),
        scratch_shapes=[
            pltpu.VMEM((count, width), BF16),
            pltpu.VMEM((ep, width), BF16),
            pltpu.VMEM((top, count), jnp.int32),
            pltpu.VMEM((count, width), BF16),
            pltpu.VMEM((ffw, width), BF16),
            pltpu.VMEM((slots, ffw), BF16),
            pltpu.VMEM((ep, count), F32),
            pltpu.VMEM((top, count), F32),
            pltpu.VMEM((ep, cap, width), BF16),
            pltpu.VMEM((ep, cap, width), BF16),
            pltpu.VMEM((rows, side, 1, 2 * count), F32),
            pltpu.VMEM((rows, side, 1, 2 * count), F32),
            pltpu.VMEM((rows, side, 1, 2 * count), F32),
            pltpu.VMEM((ep, 1, count), F32),
            pltpu.VMEM((ep, 1, count), F32),
            pltpu.VMEM((top, count), F32),
            pltpu.VMEM((edp, top, count), F32),
            pltpu.VMEM((top, count), F32),
            pltpu.VMEM((edp, top, count), F32),
            pltpu.VMEM((group, ffw), F32),
            pltpu.VMEM((rows, share, ffw), F32),
            pltpu.VMEM((share, ffw), F32),
            pltpu.VMEM((rows, share, ffw), BF16),
            pltpu.VMEM((rows, share, ffw), BF16),
            pltpu.VMEM((rows, share, ffw), BF16),
            pltpu.VMEM((rows, share, ffw), BF16),
            pltpu.VMEM((group, 128), F32),
            pltpu.VMEM((slots, width), BF16),
            pltpu.VMEM((rows, side, 1, width), F32),
            pltpu.VMEM((side, rows, 1, width), F32),
            pltpu.VMEM((rows, 1, width), F32),
            pltpu.VMEM((rows, 1, width), F32),
            dma((6,)),
            dma((2,)),
            dma,
            dma((rows,)),
            dma((4,)),
            dma((2,)),
            dma((2,)),
            dma,
            dma((rows,)),
            dma((2,)),
            dma((4,)),
        ],
        compiler_params=pltpu.CompilerParams(
            collective_id=0, has_side_effects=True, vmem_limit_bytes=60 * 1024 * 1024
        ),
    )(tokens, router_weight.T, expert_ids.T, down_weight[0], expert_hidden[0], out_grad)
    return down[None], hidden[None], router, gtok


def solution(mesh):
    in_specs = (
        P("ep", "edp"),
        P("edp", None),
        P("ep", None),
        P("ep", None, "edp"),
        P("ep", None, None),
        P("ep", "edp"),
    )
    out_specs = (P("ep", "edp", None), P("ep", "edp", None), P(("edp", "ep"), None), P("ep", "edp"))
    return jax.shard_map(
        per_device, mesh=mesh, in_specs=in_specs, out_specs=out_specs, check_vma=False
    )
```
